32 devices in a mesh: tensor: 4 (over y, core), dp: 8 (over z, x).
Axes of the slice: x: 2, y: 2, z: 4, core: 2. Of those that a mesh axis runs over, the one named last changes fastest.
Arguments:
- hidden: bfloat16 [6144, 14336], P('dp', 'tensor'), may hold values from -6 to 6
- upstream: bfloat16 [6144, 4096], P('dp'), may hold values from -4 to 4
- head_weight: bfloat16 [14, 4096], replicated, may hold values from -2 to 2
- class_probs: float32 [6144, 14], P('dp'), as said below
- teacher_votes: int32 [6144, 14], P('dp'), may hold values from 0 to 7
- clean_flag: int32 [6144], P('dp'), may hold values from 0 to 1, as said below
Outputs:
- reweighted: bfloat16 [4096, 14336], P('dp', 'tensor')
The draws below stay inside these ranges and needn't reach their ends.
Inputs may be any that keep to these rules, and one draw needn't show every extreme that they name: In each aligned block of 768 examples exactly 16 have clean_flag 1. `class_probs`: every row is positive and sums to one.
All inputs are finite; a program needn't handle non-finite values.
Results may differ from the reference program's by a relative error of at most 0.019.
Values may be sent and summed in bfloat16 or wider, within the bound.
A program may use at most 128 MiB of HBM per device.

```python
import jax
import jax.numpy as jnp
from jax import lax

D = 4096
F = 14336
CLASSES = 14
EX_DEV = 768
CLEAN_DEV = 16
EXAMPLES = 6144
CLEAN_TOT = 128
NOISY = 6016


def draw_clean_flag(key, part):
    block_keys = jax.random.split(key, EXAMPLES // EX_DEV)
    orders = jax.vmap(lambda single: jax.random.permutation(single, EX_DEV))(block_keys)
    return (orders < CLEAN_DEV).astype(jnp.int32).reshape(EXAMPLES)


def draw_class_probs(key, part):
    positive = jax.random.uniform(key, (EXAMPLES, CLASSES), jnp.float32, 0.05, 1.0)
    return positive / jnp.sum(positive, axis=1, keepdims=True)


def touch_ends(values, rng, low, top_value):
    longest = values.shape.index(max(values.shape))
    spots = []
    for shift in (0, 1):
        where = [jax.random.randint(jax.random.fold_in(rng, axis), (), 0, length) for axis, length in enumerate(values.shape)]
        where[longest] = (where[longest] + shift) % values.shape[longest]
        spots.append(tuple(where))
    return values.at[spots[0]].set(low).at[spots[1]].set(top_value)


def strengthened(array, stream_key, source, target, parts, factor):
    owner, partner = [(jnp.arange(array.shape[axis_at]) // (array.shape[axis_at] // parts)).reshape([-1 if axis == axis_at else 1 for axis in range(array.ndim)]) for axis_at in (source, target)]
    chosen = jax.random.permutation(stream_key, parts)[partner]
    strong = (owner == chosen) | (owner == (partner + parts // 2) % parts)
    return jnp.where(strong, factor * array, array)


def levels(own_key, shape, shards, least, largest):
    loudness = 1.0
    for dim, parts in shards:
        draws = jax.random.uniform(jax.random.fold_in(jax.random.fold_in(own_key, 6), dim), (parts,), jnp.float32, least / len(shards), largest / len(shards))
        loudness = loudness * jnp.repeat(jnp.exp(draws), shape[dim] // parts).reshape((-1,) + (1,) * (len(shape) - 1 - dim))
    return loudness


def bell_draw(own_key, shape, scale, reach, pieces=(), kind=jnp.bfloat16):
    result = jax.random.normal(own_key, shape, jnp.float32) * scale
    if len(pieces) > 0:
        result = levels(own_key, shape, pieces, -0.22, 0.18) * result
    return jnp.clip(result, min=-reach, max=reach).astype(kind)


def heavy_noise(key, dims, deviation, reach, pieces, heavy, kind=jnp.bfloat16):
    drawn = deviation * jax.random.normal(key, dims, jnp.float32)
    if pieces:
        drawn = drawn * levels(key, dims, pieces, -0.22, 0.18)
    return jnp.clip(strengthened(drawn, jax.random.fold_in(key, 3), *heavy), -reach, reach).astype(kind)


def setup_inputs(seed: int = 0) -> dict:
    key_of = jax.random.split(jax.random.key(seed), 7)
    return {
        "hidden": bell_draw(key_of[0], (EXAMPLES, F), 1.0, 6.0, ((0, 8), (1, 4))),
        "upstream": heavy_noise(key_of[1], (EXAMPLES, D), 0.5, 4.0, ((0, 8),), (0, 1, 8, 2.0)),
        "head_weight": bell_draw(key_of[2], (CLASSES, D), 0.3, 2.0),
        "class_probs": draw_class_probs(jax.random.fold_in(key_of[6], 71), 0),
        "teacher_votes": touch_ends(jax.random.randint(key_of[4], (EXAMPLES, CLASSES), 0, 8), jax.random.fold_in(key_of[4], 1), 0, 7).astype(jnp.int32),
        "clean_flag": draw_clean_flag(jax.random.fold_in(key_of[6], 71), 0),
    }


def gram(left, right):
    return lax.dot_general(left, right, (((1,), (1,)), ((), ())), preferred_element_type=jnp.float32)

def reference(hidden, upstream, head_weight, class_probs, teacher_votes, clean_flag):
    labels = jnp.argmax(teacher_votes, axis=1).astype(jnp.int32)
    onehot = (labels[:, None] == jnp.arange(CLASSES, dtype=jnp.int32)[None, :]).astype(jnp.float32)
    errors = class_probs - onehot
    grad_out = (upstream.astype(jnp.float32) + jnp.dot(errors, head_weight.astype(jnp.float32), precision=lax.Precision.HIGHEST)).astype(jnp.bfloat16)
    picked = jnp.argsort(1 - clean_flag, stable=True)[:CLEAN_TOT].astype(jnp.int32)
    clean_hidden = hidden[picked]
    clean_grad = grad_out[picked]
    blocks = EXAMPLES // EX_DEV
    hidden_blocks = hidden.reshape(blocks, EX_DEV, F)
    grad_blocks = grad_out.reshape(blocks, EX_DEV, D)

    def block_scores(pair):
        return lax.optimization_barrier(jnp.sum(gram(pair[0], clean_hidden) * gram(pair[1], clean_grad), axis=1))
    scores = lax.map(block_scores, (hidden_blocks, grad_blocks)).reshape(EXAMPLES)
    scores = scores / jnp.sqrt(jnp.float32(F) * jnp.float32(D) * jnp.float32(CLEAN_TOT))
    weights = jax.nn.softplus(scores) * (1 - clean_flag).astype(jnp.float32) / jnp.sqrt(jnp.float32(NOISY))
    weighted = (weights[:, None] * grad_out.astype(jnp.float32)).astype(jnp.bfloat16)
    weighted_blocks = weighted.reshape(blocks, EX_DEV, D)

    def accumulate(total, pair):
        partial_value = lax.dot_general(pair[0], pair[1], (((0,), (0,)), ((), ())), preferred_element_type=jnp.float32)
        return (total + partial_value.astype(jnp.bfloat16).astype(jnp.float32), None)
    total, unused = lax.scan(accumulate, jnp.zeros((D, F), jnp.float32), (weighted_blocks, hidden_blocks))
    return total.astype(jnp.bfloat16)
```

```python
import jax
import jax.numpy as jnp
from jax import lax
from jax.sharding import PartitionSpec as P

CLEAN_DEV = 16
CHUNKS = 4


def gram(left, right):
    return lax.dot_general(
        left, right, (((1,), (1,)), ((), ())), preferred_element_type=jnp.float32
    )


def gradient(upstream, errors, head_weight):
    first = lax.reduce_precision(errors, 8, 7)
    second = lax.reduce_precision(errors - first, 8, 7)
    third = errors - first - second
    terms = jnp.concatenate([first, second, third], axis=1).astype(jnp.bfloat16)
    heads = jnp.concatenate([head_weight] * 3, axis=0)
    product = jnp.dot(terms, heads, preferred_element_type=jnp.float32)
    return (upstream.astype(jnp.float32) + product).astype(jnp.bfloat16)


def exchange(array, bit):
    size = lax.axis_size("dp")
    return lax.ppermute(array, "dp", [(i, i ^ bit) for i in range(size)])


def body(hidden, upstream, head_weight, class_probs, teacher_votes, clean_flag):
    examples, units = hidden.shape
    width = upstream.shape[1]
    classes = class_probs.shape[1]
    groups = lax.axis_size("dp")
    me = lax.axis_index("dp")
    high = groups // 4
    rows = width // groups
    part = rows // CHUNKS
    low_bit, mid_bit, high_index = me % 2, (me // 2) % 2, me // 4

    partner_hidden = exchange(hidden, 2)

    labels = jnp.argmax(teacher_votes, axis=1)
    onehot = (labels[:, None] == jnp.arange(classes, dtype=jnp.int32)[None, :]).astype(jnp.float32)
    grad_out = gradient(upstream, class_probs - onehot, head_weight)

    place = jnp.arange(examples, dtype=jnp.int32)
    order = jnp.sum(jnp.where(place[None, :] <= place[:, None], clean_flag[None, :], 0), axis=1)
    slots = jnp.arange(1, CLEAN_DEV + 1, dtype=jnp.int32)
    pick = ((order[None, :] == slots[:, None]) & (clean_flag[None, :] == 1)).astype(jnp.bfloat16)
    clean_hidden = jnp.dot(pick, hidden, preferred_element_type=jnp.float32).astype(jnp.bfloat16)
    clean_grad = jnp.dot(pick, grad_out, preferred_element_type=jnp.float32).astype(jnp.bfloat16)
    all_hidden = lax.all_gather(clean_hidden, "dp", axis=0, tiled=True)
    all_grad = lax.all_gather(clean_grad, "dp", axis=0, tiled=True)

    split = grad_out.reshape(examples, high, 2, 2 * rows)
    own_half = lax.dynamic_index_in_dim(split, mid_bit, 2, keepdims=False)
    other_half = lax.dynamic_index_in_dim(split, 1 - mid_bit, 2, keepdims=False)
    other_half = other_half.reshape(examples, width // 2)
    partner_grad = exchange(other_half, 2)
    own_grad = own_half.reshape(examples, width // 2)

    local_scores = jnp.sum(gram(hidden, all_hidden) * gram(grad_out, all_grad), axis=1)
    scores = lax.psum(local_scores, "tensor")
    clean_total = groups * CLEAN_DEV
    noisy_total = groups * (examples - CLEAN_DEV)
    units_total = units * lax.axis_size("tensor")
    scores = scores / jnp.sqrt(jnp.float32(units_total) * jnp.float32(width) * jnp.float32(clean_total))
    weights = (
        jax.nn.softplus(scores)
        * (1 - clean_flag).astype(jnp.float32)
        / jnp.sqrt(jnp.float32(noisy_total))
    )
    both_weights = jnp.concatenate([weights, exchange(weights, 2)])
    both_hidden = jnp.concatenate([hidden, partner_hidden], axis=0)
    both_grad = jnp.concatenate([own_grad, partner_grad], axis=0)
    weighted = (both_weights[:, None] * both_grad.astype(jnp.float32)).astype(jnp.bfloat16)
    weighted = weighted.reshape(2 * examples, high, 2, CHUNKS, part)
    keep_all = lax.dynamic_index_in_dim(weighted, low_bit, 2, keepdims=False)
    send_all = lax.dynamic_index_in_dim(weighted, 1 - low_bit, 2, keepdims=False)

    def product(block):
        return lax.dot_general(
            block.reshape(2 * examples, high * part), both_hidden, (((0,), (0,)), ((), ())),
            preferred_element_type=jnp.float32,
        )

    pieces = []
    for chunk in range(CHUNKS):
        sent = product(send_all[:, :, chunk]).astype(jnp.bfloat16)
        arrived = exchange(sent, 1)
        total = (product(keep_all[:, :, chunk]) + arrived.astype(jnp.float32)).astype(jnp.bfloat16)
        size, bit = high, 4 * (high // 2)
        while size > 1:
            total = total.reshape(2, size // 2 * part, units)
            upper = (high_index // (size // 2)) % 2
            keep = lax.dynamic_index_in_dim(total, upper, 0, keepdims=False)
            give = lax.dynamic_index_in_dim(total, 1 - upper, 0, keepdims=False)
            arrived = exchange(give, bit)
            total = (keep.astype(jnp.float32) + arrived.astype(jnp.float32)).astype(jnp.bfloat16)
            size, bit = size // 2, bit // 2
        pieces.append(total)
    return jnp.concatenate(pieces, axis=0)


def solution(mesh):
    return jax.shard_map(
        body,
        mesh=mesh,
        in_specs=(P("dp", "tensor"), P("dp", None), P(), P("dp", None), P("dp", None), P("dp")),
        out_specs=P("dp", "tensor"),
        check_vma=False,
    )
```

```python
import jax
import jax.numpy as jnp
from jax import lax
from jax.sharding import PartitionSpec as P

CLEAN_DEV = 16
CHUNKS = 7
AHEAD = 3


def gram(left, right):
    return lax.dot_general(
        left, right, (((1,), (1,)), ((), ())), preferred_element_type=jnp.float32
    )


def gradient(upstream, errors, head_weight):
    first = lax.reduce_precision(errors, 8, 7)
    second = lax.reduce_precision(errors - first, 8, 7)
    third = errors - first - second
    terms = jnp.concatenate([first, second, third], axis=1).astype(jnp.bfloat16)
    heads = jnp.concatenate([head_weight] * 3, axis=0)
    product = jnp.dot(terms, heads, preferred_element_type=jnp.float32)
    return (upstream.astype(jnp.float32) + product).astype(jnp.bfloat16)


def exchange(array, bit, axis="dp"):
    size = lax.axis_size(axis)
    return lax.ppermute(array, axis, [(i, i ^ bit) for i in range(size)])


def after(value, *others):
    return lax.optimization_barrier((value, *others))[0]


def choose(bit, zero, one):
    return jnp.where(bit == 0, zero, one)


def spread(piece):
    me = lax.axis_index("tensor")
    bit = lax.axis_size("tensor") // 2
    while bit:
        other = exchange(piece, bit, "tensor")
        mine = (me // bit) % 2
        piece = jnp.concatenate([choose(mine, piece, other), choose(mine, other, piece)], axis=0)
        bit //= 2
    return piece


def bit_reversed(size):
    me = lax.axis_index("tensor")
    result, bit = 0, size // 2
    place = 1
    while bit:
        result = result + ((me // bit) % 2) * place
        bit, place = bit // 2, place * 2
    return result


def body(hidden, upstream, head_weight, class_probs, teacher_votes, clean_flag):
    examples, units = hidden.shape
    width = upstream.shape[1]
    classes = class_probs.shape[1]
    groups = lax.axis_size("dp")
    tensors = lax.axis_size("tensor")
    me = lax.axis_index("dp")
    high = groups // 4
    rows = width // groups
    low_bit, mid_bit, high_index = me % 2, (me // 2) % 2, me // 4
    chunk = units // CHUNKS

    def columns(index):
        return hidden[:, index * chunk:(index + 1) * chunk]

    arrived_hidden = [exchange(columns(0), 2)]

    labels = jnp.argmax(teacher_votes, axis=1)
    onehot = (labels[:, None] == jnp.arange(classes, dtype=jnp.int32)[None, :]).astype(jnp.float32)
    grad_out = gradient(upstream, class_probs - onehot, head_weight)

    place = jnp.arange(examples, dtype=jnp.int32)
    order = jnp.sum(jnp.where(place[None, :] <= place[:, None], clean_flag[None, :], 0), axis=1)
    slots = jnp.arange(1, CLEAN_DEV + 1, dtype=jnp.int32)
    pick = ((order[None, :] == slots[:, None]) & (clean_flag[None, :] == 1)).astype(jnp.bfloat16)
    clean_hidden = jnp.dot(pick, hidden, preferred_element_type=jnp.float32).astype(jnp.bfloat16)
    clean_grad = jnp.dot(pick, grad_out, preferred_element_type=jnp.float32).astype(jnp.bfloat16)
    clean = jnp.concatenate([clean_hidden, clean_grad], axis=1)
    gathered = lax.all_gather(clean, "dp", axis=0, tiled=True)
    all_hidden, all_grad = gathered[:, :units], gathered[:, units:]

    def half(array, mid):
        return jnp.concatenate(
            [array[:, (4 * h + 2 * mid) * rows:(4 * h + 2 * mid + 2) * rows] for h in range(high)], axis=1
        )

    share = examples // tensors
    own_rows = lax.dynamic_slice_in_dim(grad_out, bit_reversed(tensors) * share, share, 0)
    shipped = choose(mid_bit, half(own_rows, 1), half(own_rows, 0))
    partner_grad = spread(exchange(after(shipped, gathered), 2))
    own_grad = choose(mid_bit, half(grad_out, 0), half(grad_out, 1))

    for index in range(1, AHEAD):
        arrived_hidden.append(exchange(after(columns(index), gathered), 2))

    local_scores = jnp.sum(gram(hidden, all_hidden) * gram(grad_out, all_grad), axis=1)
    scores = lax.psum(local_scores, "tensor")
    clean_total = groups * CLEAN_DEV
    noisy_total = groups * (examples - CLEAN_DEV)
    scores = scores / jnp.sqrt(jnp.float32(units * tensors) * jnp.float32(width) * jnp.float32(clean_total))
    weights = (
        jax.nn.softplus(scores)
        * (1 - clean_flag).astype(jnp.float32)
        / jnp.sqrt(jnp.float32(noisy_total))
    )
    partner_weights = exchange(weights, 2)

    def scaled(factor, array):
        return (factor[:, None] * array.astype(jnp.float32)).astype(jnp.bfloat16)

    weighted = jnp.concatenate([scaled(weights, own_grad), scaled(partner_weights, partner_grad)], axis=0)

    def side(low):
        return jnp.concatenate(
            [weighted[:, (2 * h + low) * rows:(2 * h + low + 1) * rows] for h in range(high)], axis=1
        )

    keep_side = choose(low_bit, side(0), side(1))
    send_side = choose(low_bit, side(1), side(0))

    def product(left, right):
        return lax.dot_general(
            left, right, (((0,), (0,)), ((), ())), preferred_element_type=jnp.float32
        )

    def begin(index):
        rights.append(jnp.concatenate([columns(index), arrived_hidden[index]], axis=0))
        sent = product(send_side, rights[index]).astype(jnp.bfloat16)
        arrived_rows.append(exchange(sent, 1))
        if len(arrived_hidden) < CHUNKS:
            arrived_hidden.append(exchange(after(columns(len(arrived_hidden)), sent), 2))

    pieces, rights, arrived_rows = [], [], []
    for index in range(AHEAD):
        begin(index)
    for index in range(CHUNKS):
        right, arrived = rights[index], arrived_rows[index]
        total = (product(keep_side, right) + arrived.astype(jnp.float32)).astype(jnp.bfloat16)
        size, bit = high, 4 * (high // 2)
        while size > 1:
            middle = size // 2 * rows
            upper = (high_index // (size // 2)) % 2
            give = choose(upper, total[middle:], total[:middle])
            if size == high and index + AHEAD < CHUNKS:
                give, arrived_hidden[index + AHEAD] = lax.optimization_barrier((give, arrived_hidden[index + AHEAD]))
            arrived = exchange(give, bit)
            keep = choose(upper, total[:middle], total[middle:])
            if size > 2:
                total = (keep.astype(jnp.float32) + arrived.astype(jnp.float32)).astype(jnp.bfloat16)
            size, bit = size // 2, bit // 2
        pieces.append((keep, arrived))
        if index + AHEAD < CHUNKS:
            begin(index + AHEAD)
    finished = [keep.astype(jnp.float32) + after(arrived, give).astype(jnp.float32) for keep, arrived in pieces[:-1]]
    keep, arrived = pieces[-1]
    finished.append(keep.astype(jnp.float32) + arrived.astype(jnp.float32))
    return jnp.concatenate([total.astype(jnp.bfloat16) for total in finished], axis=1)


def solution(mesh):
    return jax.shard_map(
        body,
        mesh=mesh,
        in_specs=(P("dp", "tensor"), P("dp", None), P(), P("dp", None), P("dp", None), P("dp")),
        out_specs=P("dp", "tensor"),
        check_vma=False,
    )
```

```python
import jax
import jax.numpy as jnp
from jax import lax
from jax.sharding import PartitionSpec as P

CLEAN_DEV = 16
CHUNKS = 7
AHEAD = 3


def gram(left, right):
    return lax.dot_general(
        left, right, (((1,), (1,)), ((), ())), preferred_element_type=jnp.float32
    )


def gradient(upstream, errors, head_weight):
    first = lax.reduce_precision(errors, 8, 7)
    second = lax.reduce_precision(errors - first, 8, 7)
    third = errors - first - second
    terms = jnp.concatenate([first, second, third], axis=1).astype(jnp.bfloat16)
    heads = jnp.concatenate([head_weight] * 3, axis=0)
    product = jnp.dot(terms, heads, preferred_element_type=jnp.float32)
    return (upstream.astype(jnp.float32) + product).astype(jnp.bfloat16)


def exchange(array, bit, axis="dp"):
    size = lax.axis_size(axis)
    return lax.ppermute(array, axis, [(i, i ^ bit) for i in range(size)])


def after(value, *others):
    return lax.optimization_barrier((value, *others))[0]


def choose(bit, zero, one):
    return jnp.where(bit == 0, zero, one)


def spread(piece):
    me = lax.axis_index("tensor")
    bit = lax.axis_size("tensor") // 2
    while bit:
        other = exchange(piece, bit, "tensor")
        mine = (me // bit) % 2
        piece = jnp.concatenate([choose(mine, piece, other), choose(mine, other, piece)], axis=0)
        bit //= 2
    return piece


def bit_reversed(size):
    me = lax.axis_index("tensor")
    result, bit = 0, size // 2
    place = 1
    while bit:
        result = result + ((me // bit) % 2) * place
        bit, place = bit // 2, place * 2
    return result


def body(hidden, upstream, head_weight, class_probs, teacher_votes, clean_flag):
    examples, units = hidden.shape
    width = upstream.shape[1]
    classes = class_probs.shape[1]
    groups = lax.axis_size("dp")
    tensors = lax.axis_size("tensor")
    me = lax.axis_index("dp")
    high = groups // 4
    rows = width // groups
    low_bit, mid_bit, high_index = me % 2, (me // 2) % 2, me // 4
    step = units // CHUNKS
    edges = [index * step for index in range(CHUNKS)] + [units - step // 2, units]
    chunks = len(edges) - 1

    first_columns = lax.optimization_barrier(hidden[:, :step])
    arrived_hidden = [exchange(first_columns, 2)]

    labels = jnp.argmax(teacher_votes, axis=1)
    onehot = (labels[:, None] == jnp.arange(classes, dtype=jnp.int32)[None, :]).astype(jnp.float32)
    grad_out = gradient(upstream, class_probs - onehot, head_weight)

    place = jnp.arange(examples, dtype=jnp.int32)
    order = jnp.sum(jnp.where(place[None, :] <= place[:, None], clean_flag[None, :], 0), axis=1)
    slots = jnp.arange(1, CLEAN_DEV + 1, dtype=jnp.int32)
    pick = ((order[None, :] == slots[:, None]) & (clean_flag[None, :] == 1)).astype(jnp.bfloat16)
    clean_hidden = jnp.dot(pick, hidden, preferred_element_type=jnp.float32).astype(jnp.bfloat16)
    clean_grad = jnp.dot(pick, grad_out, preferred_element_type=jnp.float32).astype(jnp.bfloat16)
    clean = jnp.concatenate([clean_hidden, clean_grad], axis=1)
    gathered = lax.all_gather(clean, "dp", axis=0, tiled=True)
    all_hidden, all_grad = gathered[:, :units], gathered[:, units:]

    def half(array, mid):
        return jnp.concatenate(
            [array[:, (4 * h + 2 * mid) * rows:(4 * h + 2 * mid + 2) * rows] for h in range(high)], axis=1
        )

    share = examples // tensors
    own_rows = lax.dynamic_slice_in_dim(grad_out, bit_reversed(tensors) * share, share, 0)
    shipped = choose(mid_bit, half(own_rows, 1), half(own_rows, 0))
    shipped = exchange(after(shipped, gathered), 2)
    own_grad = choose(mid_bit, half(grad_out, 0), half(grad_out, 1))

    local_scores = jnp.sum(gram(hidden, all_hidden) * gram(grad_out, all_grad), axis=1)
    partner_grad = spread(after(shipped, local_scores))
    held = after(hidden, gathered)

    def columns(index):
        return held[:, edges[index]:edges[index + 1]] if index else first_columns

    for index in range(1, AHEAD):
        arrived_hidden.append(exchange(after(columns(index), local_scores), 2))
    scores = lax.psum(local_scores, "tensor")
    clean_total = groups * CLEAN_DEV
    noisy_total = groups * (examples - CLEAN_DEV)
    scores = scores / jnp.sqrt(jnp.float32(units * tensors) * jnp.float32(width) * jnp.float32(clean_total))
    weights = (
        jax.nn.softplus(scores)
        * (1 - clean_flag).astype(jnp.float32)
        / jnp.sqrt(jnp.float32(noisy_total))
    )
    partner_weights = exchange(weights, 2)

    def scaled(factor, array):
        return (factor[:, None] * array.astype(jnp.float32)).astype(jnp.bfloat16)

    weighted = jnp.concatenate([scaled(weights, own_grad), scaled(partner_weights, partner_grad)], axis=0)

    def side(low):
        return jnp.concatenate(
            [weighted[:, (2 * h + low) * rows:(2 * h + low + 1) * rows] for h in range(high)], axis=1
        )

    keep_side = choose(low_bit, side(0), side(1))
    send_side = choose(low_bit, side(1), side(0))

    def product(left, right):
        return lax.dot_general(
            left, right, (((0,), (0,)), ((), ())), preferred_element_type=jnp.float32
        )

    def begin(index):
        rights.append(jnp.concatenate([columns(index), arrived_hidden[index]], axis=0))
        sent = product(send_side, rights[index]).astype(jnp.bfloat16)
        arrived_rows.append(exchange(sent, 1))
        if len(arrived_hidden) < chunks:
            arrived_hidden.append(exchange(after(columns(len(arrived_hidden)), sent), 2))

    pieces, gives, rights, arrived_rows = [], [], [], []
    for index in range(AHEAD):
        begin(index)
    for index in range(chunks):
        right, arrived = rights[index], arrived_rows[index]
        if index:
            arrived = after(arrived, gives[-1])
        total = (product(keep_side, right) + arrived.astype(jnp.float32)).astype(jnp.bfloat16)
        size, bit = high, 4 * (high // 2)
        while size > 1:
            middle = size // 2 * rows
            upper = (high_index // (size // 2)) % 2
            give = choose(upper, total[middle:], total[:middle])
            if size == high and index + AHEAD < chunks:
                give, arrived_hidden[index + AHEAD] = lax.optimization_barrier((give, arrived_hidden[index + AHEAD]))
            arrived = exchange(give, bit)
            keep = choose(upper, total[:middle], total[middle:])
            if size > 2:
                total = (keep.astype(jnp.float32) + arrived.astype(jnp.float32)).astype(jnp.bfloat16)
            size, bit = size // 2, bit // 2
        pieces.append((keep, arrived))
        gives.append(give)
        if index + AHEAD < chunks:
            begin(index + AHEAD)
    finished = []
    for index, (keep, arrived) in enumerate(pieces):
        if index < chunks - 1:
            arrived = after(arrived, gives[min(index + 2, chunks - 1)])
        finished.append(keep.astype(jnp.float32) + arrived.astype(jnp.float32))
    return jnp.concatenate([total.astype(jnp.bfloat16) for total in finished], axis=1)


def solution(mesh):
    return jax.shard_map(
        body,
        mesh=mesh,
        in_specs=(P("dp", "tensor"), P("dp", None), P(), P("dp", None), P("dp", None), P("dp")),
        out_specs=P("dp", "tensor"),
        check_vma=False,
    )
```

```python
import jax
import jax.numpy as jnp
from jax import lax
from jax.sharding import PartitionSpec as P

CLEAN_DEV = 16
CHUNKS = 7
AHEAD = 3


def gram(left, right):
    return lax.dot_general(
        left, right, (((1,), (1,)), ((), ())), preferred_element_type=jnp.float32
    )


def gradient(upstream, errors, head_weight):
    first = lax.reduce_precision(errors, 8, 7)
    second = lax.reduce_precision(errors - first, 8, 7)
    third = errors - first - second
    terms = jnp.concatenate([first, second, third], axis=1).astype(jnp.bfloat16)
    heads = jnp.concatenate([head_weight] * 3, axis=0)
    product = jnp.dot(terms, heads, preferred_element_type=jnp.float32)
    return (upstream.astype(jnp.float32) + product).astype(jnp.bfloat16)


def exchange(array, bit, axis="dp"):
    size = lax.axis_size(axis)
    return lax.ppermute(array, axis, [(i, i ^ bit) for i in range(size)])


def after(value, *others):
    return lax.optimization_barrier((value, *others))[0]


def choose(bit, zero, one):
    return jnp.where(bit == 0, zero, one)


def spread(piece):
    me = lax.axis_index("tensor")
    bit = lax.axis_size("tensor") // 2
    while bit:
        other = exchange(piece, bit, "tensor")
        mine = (me // bit) % 2
        piece = jnp.concatenate([choose(mine, piece, other), choose(mine, other, piece)], axis=0)
        bit //= 2
    return piece


def bit_reversed(size):
    me = lax.axis_index("tensor")
    result, bit = 0, size // 2
    place = 1
    while bit:
        result = result + ((me // bit) % 2) * place
        bit, place = bit // 2, place * 2
    return result


def body(hidden, upstream, head_weight, class_probs, teacher_votes, clean_flag):
    examples, units = hidden.shape
    width = upstream.shape[1]
    classes = class_probs.shape[1]
    groups = lax.axis_size("dp")
    tensors = lax.axis_size("tensor")
    me = lax.axis_index("dp")
    high = groups // 4
    rows = width // groups
    low_bit, mid_bit, high_index = me % 2, (me // 2) % 2, me // 4
    step = units // CHUNKS
    edges = [index * step for index in range(CHUNKS)] + [units - step // 2, units]
    chunks = len(edges) - 1

    first_columns = lax.optimization_barrier(hidden[:, :step])
    arrived_hidden = [exchange(first_columns, 2)]

    labels = jnp.argmax(teacher_votes, axis=1)
    onehot = (labels[:, None] == jnp.arange(classes, dtype=jnp.int32)[None, :]).astype(jnp.float32)
    grad_out = gradient(upstream, class_probs - onehot, head_weight)

    place = jnp.arange(examples, dtype=jnp.int32)
    order = jnp.sum(jnp.where(place[None, :] <= place[:, None], clean_flag[None, :], 0), axis=1)
    slots = jnp.arange(1, CLEAN_DEV + 1, dtype=jnp.int32)
    pick = ((order[None, :] == slots[:, None]) & (clean_flag[None, :] == 1)).astype(jnp.bfloat16)
    clean_hidden = jnp.dot(pick, hidden, preferred_element_type=jnp.float32).astype(jnp.bfloat16)
    clean_grad = jnp.dot(pick, grad_out, preferred_element_type=jnp.float32).astype(jnp.bfloat16)
    clean = jnp.concatenate([clean_hidden, clean_grad], axis=1)
    gathered = lax.all_gather(clean, "dp", axis=0, tiled=True)

    def half(array, mid):
        return jnp.concatenate(
            [array[:, (4 * h + 2 * mid) * rows:(4 * h + 2 * mid + 2) * rows] for h in range(high)], axis=1
        )

    share = examples // tensors
    own_rows = lax.dynamic_slice_in_dim(grad_out, bit_reversed(tensors) * share, share, 0)
    shipped = choose(mid_bit, half(own_rows, 1), half(own_rows, 0))
    received = exchange(after(shipped, clean), 2)
    own_grad = choose(mid_bit, half(grad_out, 0), half(grad_out, 1))
    gathered, received, own_grad, arrived_hidden[0] = lax.optimization_barrier(
        (gathered, received, own_grad, arrived_hidden[0])
    )
    partner_grad = spread(received)
    all_hidden, all_grad = gathered[:, :units], gathered[:, units:]

    local_scores = jnp.sum(gram(hidden, all_hidden) * gram(grad_out, all_grad), axis=1)
    held = after(hidden, gathered)

    def columns(index):
        return held[:, edges[index]:edges[index + 1]] if index else first_columns

    for index in range(1, AHEAD):
        arrived_hidden.append(exchange(after(columns(index), gathered), 2))
    scores = lax.psum(local_scores, "tensor")
    clean_total = groups * CLEAN_DEV
    noisy_total = groups * (examples - CLEAN_DEV)
    scores = scores / jnp.sqrt(jnp.float32(units * tensors) * jnp.float32(width) * jnp.float32(clean_total))
    weights = (
        jax.nn.softplus(scores)
        * (1 - clean_flag).astype(jnp.float32)
        / jnp.sqrt(jnp.float32(noisy_total))
    )
    partner_weights = exchange(weights, 2)

    def scaled(factor, array):
        return (factor[:, None] * array.astype(jnp.float32)).astype(jnp.bfloat16)

    weighted = jnp.concatenate([scaled(weights, own_grad), scaled(partner_weights, partner_grad)], axis=0)

    def side(low):
        return jnp.concatenate(
            [weighted[:, (2 * h + low) * rows:(2 * h + low + 1) * rows] for h in range(high)], axis=1
        )

    keep_side = choose(low_bit, side(0), side(1))
    send_side = choose(low_bit, side(1), side(0))

    def product(left, right):
        return lax.dot_general(
            left, right, (((0,), (0,)), ((), ())), preferred_element_type=jnp.float32
        )

    def begin(index):
        rights.append(jnp.concatenate([columns(index), arrived_hidden[index]], axis=0))
        sent = product(send_side, rights[index]).astype(jnp.bfloat16)
        arrived_rows.append(exchange(sent, 1))
        if len(arrived_hidden) < chunks:
            arrived_hidden.append(exchange(after(columns(len(arrived_hidden)), sent), 2))

    pieces, gives, rights, arrived_rows = [], [], [], []
    for index in range(AHEAD):
        begin(index)
    for index in range(chunks):
        right, arrived = rights[index], arrived_rows[index]
        if index:
            arrived = after(arrived, gives[-1])
        total = (product(keep_side, right) + arrived.astype(jnp.float32)).astype(jnp.bfloat16)
        size, bit = high, 4 * (high // 2)
        while size > 1:
            middle = size // 2 * rows
            upper = (high_index // (size // 2)) % 2
            give = choose(upper, total[middle:], total[:middle])
            if size == high and index + AHEAD < chunks:
                give, arrived_hidden[index + AHEAD] = lax.optimization_barrier((give, arrived_hidden[index + AHEAD]))
            arrived = exchange(give, bit)
            keep = choose(upper, total[:middle], total[middle:])
            if size > 2:
                total = (keep.astype(jnp.float32) + arrived.astype(jnp.float32)).astype(jnp.bfloat16)
            size, bit = size // 2, bit // 2
        pieces.append((keep, arrived))
        gives.append(give)
        if index + AHEAD < chunks:
            begin(index + AHEAD)
    finished = []
    for index, (keep, arrived) in enumerate(pieces):
        if index < chunks - 1:
            arrived = after(arrived, gives[min(index + 2, chunks - 1)])
        finished.append(keep.astype(jnp.float32) + arrived.astype(jnp.float32))
    return jnp.concatenate([total.astype(jnp.bfloat16) for total in finished], axis=1)


def solution(mesh):
    return jax.shard_map(
        body,
        mesh=mesh,
        in_specs=(P("dp", "tensor"), P("dp", None), P(), P("dp", None), P("dp", None), P("dp")),
        out_specs=P("dp", "tensor"),
        check_vma=False,
    )
```
